256 devices in a mesh: rep: 8 (over z), own: 32 (over x, y, core).
Axes of the slice: x: 4, y: 4, z: 8, core: 2. Of those that a mesh axis runs over, the one named last changes fastest.
Arguments:
- lambda_amp: float32 [8192, 3072], P('own', 'rep'), may hold values from -7 to 7
- lambda_tiles: int32 [8192, 24], P('own', 'rep'), may hold values 0 or 1
- integrals: float32 [3072, 3072], P(('rep', 'own')), may hold values from -100 to 100
- integral_tiles: int32 [24, 24], replicated, may hold values 0 or 1
Outputs:
- residual: float32 [8192, 3072], P('own', 'rep')
The draws below stay inside these ranges and needn't reach their ends.
All inputs are finite; a program needn't handle non-finite values. No bound on the sum of `lambda_tiles` on one device may be relied on, other than what follows from the above.
Results may differ from the reference program's by a relative error of at most 0.0003.
Values may be sent and summed in bfloat16 or wider, within the bound.
A program may use at most 64 MiB of HBM per device.

```python
import jax
import jax.numpy as jnp
from jax import lax

TILE = 128
VT = 24
NV = 3072
ROWS = 8192


def column_places(key):
    base = jnp.broadcast_to(jnp.arange(TILE, dtype=jnp.int32)[None, :], (VT, TILE))
    order = jax.random.permutation(jax.random.fold_in(key, 101), base, axis=1, independent=True)
    return jnp.argsort(order, axis=1).astype(jnp.int32)


def draw_lambda_amp(key, part):
    places = column_places(key)
    key = jax.random.fold_in(key, 11)
    first_key, second_key = jax.random.split(key)
    half = TILE // 2
    shape = (ROWS, VT, half)
    base = jnp.clip(jax.random.normal(first_key, shape, jnp.float32), -6.0, 6.0)
    shift = jnp.clip(jax.random.normal(second_key, shape, jnp.float32), -6.0, 6.0)
    factor = 256.0
    ordered = jnp.concatenate([base, base + shift / factor], axis=2)
    index = jnp.broadcast_to(places[None, :, :], (ROWS, VT, TILE))
    values = jnp.take_along_axis(ordered, index, axis=2)
    return values.reshape(ROWS, NV)


def draw_integrals(key, part):
    places = column_places(key)
    key = jax.random.fold_in(key, 23)
    first_key, second_key = jax.random.split(key)
    half = TILE // 2
    shape = (VT, half, NV)
    norm = NV ** (-0.5)
    major = jnp.clip(jax.random.normal(first_key, shape, jnp.float32), -6.0, 6.0)
    minor = jnp.clip(jax.random.normal(second_key, shape, jnp.float32), -6.0, 6.0)
    factor = 256.0
    large = major * (factor * norm)
    ordered = jnp.concatenate([large, minor * norm - large], axis=1)
    index = jnp.broadcast_to(places[:, :, None], (VT, TILE, NV))
    values = jnp.take_along_axis(ordered, index, axis=1)
    return values.reshape(NV, NV)


def with_ends(drawn, key, low, largest):
    place = [jax.random.randint(jax.random.fold_in(key, axis), (), 0, length) for axis, length in enumerate(drawn.shape)]
    main_axis = drawn.shape.index(max(drawn.shape))
    neighbour = place[:main_axis] + [(place[main_axis] + 1) % drawn.shape[main_axis]] + place[main_axis + 1:]
    return drawn.at[tuple(place)].set(low).at[tuple(neighbour)].set(largest)


def setup_inputs(seed: int = 0) -> dict:
    splits = jax.random.split(jax.random.key(seed), 5)
    lambda_amp = draw_lambda_amp(jax.random.fold_in(splits[4], 71), 0)
    lambda_tiles = with_ends((jax.random.randint(splits[1], (ROWS, VT), 0, 2) < 1).astype(jnp.int32), jax.random.fold_in(splits[1], 1), 0, 1)
    integrals = draw_integrals(jax.random.fold_in(splits[4], 71), 0)
    integral_tiles = with_ends((jax.random.randint(splits[3], (VT, VT), 0, 4) < 3).astype(jnp.int32), jax.random.fold_in(splits[3], 1), 0, 1)
    return dict(lambda_amp=lambda_amp, lambda_tiles=lambda_tiles, integrals=integrals, integral_tiles=integral_tiles)


def split_three(values):
    first = values.astype(jnp.bfloat16)
    first_wide = lax.optimization_barrier(first).astype(jnp.float32)
    rest = values - first_wide
    second = rest.astype(jnp.bfloat16)
    second_wide = lax.optimization_barrier(second).astype(jnp.float32)
    rest = rest - second_wide
    third = rest.astype(jnp.bfloat16)
    return first, second, third


def slice_product(left, right):
    pairs = ((0, 0), (0, 1), (1, 0), (0, 2), (1, 1), (2, 0))
    total = jnp.dot(left[0], right[0], preferred_element_type=jnp.float32)
    for first, second in pairs[1:]:
        total = total + jnp.dot(left[first], right[second], preferred_element_type=jnp.float32)
    return total


def reference(lambda_amp, lambda_tiles, integrals, integral_tiles):
    keep = jnp.repeat(lambda_tiles.astype(jnp.float32), TILE, axis=1)
    left = split_three(lambda_amp * keep)
    block_mask = jnp.repeat(jnp.repeat(integral_tiles.astype(jnp.float32), TILE, axis=0), TILE, axis=1)
    right = split_three(integrals * block_mask)
    return slice_product(left, right)
```

```python
import jax
import jax.numpy as jnp
from jax import lax
from jax.experimental import pallas as pl
from jax.experimental.pallas import tpu as pltpu
from jax.sharding import PartitionSpec as P

MESH = pl.DeviceIdType.MESH
F32, BF16, I32, I16 = jnp.float32, jnp.bfloat16, jnp.int32, jnp.int16
TILE = 128
W = 384
ROWS = 256
SUB = 128
Q = 32767.0


def split3(v):
    first = v.astype(BF16)
    rest = v - first.astype(F32)
    second = rest.astype(BF16)
    rest = rest - second.astype(F32)
    return first, second, rest.astype(BF16)


def encode(v):
    top = jnp.maximum(jnp.max(jnp.abs(v), axis=0, keepdims=True), 1e-30)
    code = jnp.round(v * (Q / top)).astype(I32).astype(I16)
    return code, top * (1.0 / Q)


def decode(code, scale):
    return code.astype(I32).astype(F32) * scale


def kernel(
    lam_hbm, keep_hbm, ints_hbm, flags, out,
    lam, keep, ints, lamx, ge, he, gp, hp, la, lb, ra, part, own_part,
    sq, ss, rq, rs, fq, fs,
    in_sem, s1, r1, s2, r2, sf, rf, sl, rl, szq, szs, rzq, rzs, rfq, rfs,
):
    z = lax.axis_index("rep")
    own = lax.axis_index("own")
    core = lax.rem(own, 2)
    x = own // 8
    y = lax.rem(own // 2, 4)
    a = x + core * (y - x)
    b = y + core * (x - y)
    step = 1 - 2 * core

    def at(dz, da, db, c):
        aa, bb = lax.rem(a + da, 4), lax.rem(b + db, 4)
        xx, yy = aa + core * (bb - aa), bb + core * (aa - bb)
        return (lax.rem(z + dz + 8, 8), (xx * 4 + yy) * 2 + c)

    def chunk(distance, c):
        return lax.rem(z + distance * (1 - 2 * c) + 8, 8)

    def remote(src, dst, send, recv, device):
        return pltpu.make_async_remote_copy(
            src_ref=src, dst_ref=dst, send_sem=send, recv_sem=recv, device_id=device, device_id_type=MESH
        )

    loads = [
        pltpu.make_async_copy(ints_hbm, ints, in_sem.at[0]),
        pltpu.make_async_copy(lam_hbm, lam, in_sem.at[1]),
        pltpu.make_async_copy(keep_hbm, keep, in_sem.at[2]),
    ]
    for load in loads:
        load.start()

    barrier = pltpu.get_barrier_semaphore()
    peers = [at(0, 0, 0, 1 - core)]
    peers += [at(0, t, 0, core) for t in (1, 2, 3)] + [at(0, 0, t, core) for t in (1, 2, 3)]
    peers += [at(step, 0, 0, core), at(-step, 0, 0, core), at(step, 0, 0, 1 - core)]
    for peer in peers:
        pl.semaphore_signal(barrier, inc=1, device_id=peer, device_id_type=MESH)

    loads[0].wait()
    first_row = own * 12
    t0 = first_row // TILE
    t1 = (first_row + 11) // TILE
    bound = (t0 + 1) * TILE - first_row
    above = lax.broadcasted_iota(I32, (12, TILE), 0) < bound
    for j in range(24):
        f0 = flags[3 * z + t0, j].astype(F32)
        f1 = flags[3 * z + t1, j].astype(F32)
        ints[:, j * TILE : (j + 1) * TILE] = ints[:, j * TILE : (j + 1) * TILE] * jnp.where(above, f0, f1)

    def columns(ch):
        return pl.ds(pl.multiple_of(ch * W, TILE), W)

    for e, distance in ((0, 4), (1, 0)):
        cols = columns(chunk(distance, core))
        ge[e, a, b, 0] = ints[0:8, cols]
        ge[e, a, b, 1, 0:4] = ints[8:12, cols]
        ge[e, a, b, 1, 4:8] = ints[8:12, cols]
    for p in range(3):
        gp[p, a, b, 0] = ints[0:8, columns(chunk(3 - p, 0))]
        gp[p, a, b, 2] = ints[0:8, columns(chunk(3 - p, 1))]
        gp[p, a, b, 1, 0:4] = ints[8:12, columns(chunk(3 - p, core))]
        gp[p, a, b, 1, 4:8] = ints[8:12, columns(chunk(3 - p, 1 - core))]

    loads[1].wait()
    loads[2].wait()
    for u in range(3):
        cols = slice(u * TILE, (u + 1) * TILE)
        lam[:, cols] = lam[:, cols] * keep[:, u : u + 1].astype(F32)

    def gathered(g):
        return ge.at[(0, None, None, None, 1)[g]] if g in (0, 4) else gp.at[g - 1]

    def handed(g):
        return he.at[(0, None, None, None, 1)[g]] if g in (0, 4) else hp.at[g - 1]

    def phase1(g, t):
        mine = gathered(g).at[a, b]
        return remote(mine, mine, s1.at[g, t - 1], r1.at[g, t - 1], at(0, 0, t, core))

    def phase2(g, t):
        mine = gathered(g).at[a]
        return remote(mine, mine, s2.at[g, t - 1], r2.at[g, t - 1], at(0, t, 0, core))

    def handing(g, t):
        aa = lax.rem(a + 4 - t, 4)
        if g in (0, 4):
            src = gathered(g).at[aa]
        else:
            src = gathered(g).at[aa, :, pl.ds(1 - core, 2)]
        return remote(src, handed(g).at[aa], sf.at[g, t], rf.at[g, t], at(0, 0, 0, 1 - core))

    def start1(g):
        for t in (1, 3, 2):
            phase1(g, t).start()

    def start2(g):
        for t in (1, 3, 2):
            phase1(g, t).wait_recv()
        for t in (1, 3, 2):
            phase2(g, t).start()
        handing(g, 0).start()

    def hand(g):
        for t in (1, 3, 2):
            phase2(g, t).wait_recv()
            handing(g, t).start()

    def arrived(g):
        for t in range(4):
            handing(g, t).wait_recv()

    lam_copy = remote(lam, lamx, sl, rl, at(0, 0, 0, 1 - core))

    pl.semaphore_wait(barrier, len(peers))
    start1(0)
    lam_copy.start()
    start1(1)

    n = lax.broadcasted_iota(I32, (1, W), 1)
    m = n & 127
    ia, ib, r = m >> 5, (m >> 3) & 3, m & 7
    up, down = ia * 4 + ib, ib * 4 + ia
    mine = 24 * (up + core * (down - up)) + 12 * core
    theirs = 24 * (down + core * (up - down)) + 12 * (1 - core)
    tail = jnp.where(r < 4, mine + 8 + r, theirs + 4 + r)
    place = jnp.where(n < 128, mine + r, jnp.where(n < 256, theirs + r, tail))
    order = (lax.broadcasted_iota(I32, (W, W), 0) == place).astype(BF16)

    def prepare(values, h):
        rows = slice(h * ROWS, (h + 1) * ROWS)
        l1, l2, l3 = (jnp.dot(s, order, preferred_element_type=F32).astype(BF16) for s in split3(values))
        for i, s in enumerate((l1, l1, l1, l3)):
            la[rows, i * W : (i + 1) * W] = s
        for i in range(2):
            lb[rows, i * W : (i + 1) * W] = l2

    prepare(lam[...], 0)
    start2(0)
    start1(2)
    start1(3)
    start1(4)
    start2(1)
    lam_copy.wait_recv()
    prepare(lamx[...], 1)

    def right(g):
        if g in (0, 4):
            mine, theirs = gathered(g), handed(g)
            places = (0, 1), (0, 1)
        else:
            mine, theirs = gathered(g), handed(g)
            places = (2 * core, 1), (core, 1 - core)
        low = lax.broadcasted_iota(I32, (16, 8, W), 1) < 4

        def piece(ref, place):
            return ref[:, :, place].reshape(16, 8, W)

        parts = (
            piece(mine, places[0][0]),
            piece(theirs, places[1][0]),
            jnp.where(low, piece(mine, places[0][1]), piece(theirs, places[1][1])),
        )
        for i, v in enumerate(parts):
            r1_, r2_, r3_ = split3(v.reshape(128, W))
            for k, s in enumerate((r1_, r2_, r3_, r1_)):
                ra[k * W + i * 128 : k * W + (i + 1) * 128] = s

    def product(h):
        rows = slice(h * ROWS, (h + 1) * ROWS)
        total = jnp.dot(la[rows], ra[...], preferred_element_type=F32)
        return total + jnp.dot(lb[rows], ra[0 : 2 * W], preferred_element_type=F32)

    def sends(j, h, u):
        if j < 3:
            target = at(step, 0, 0, core)
            to = (rq.at[j, h, u], rs.at[j, h, u], rzq.at[j, h, u], rzs.at[j, h, u])
        else:
            target = at(step, 0, 0, core if h == 0 else 1 - core)
            to = (fq.at[core, u], fs.at[core, u], rfq.at[core, u], rfs.at[core, u])
        return (
            remote(sq.at[j, h, u], to[0], szq.at[j, h, u], to[2], target),
            remote(ss.at[j, h, u], to[1], szs.at[j, h, u], to[3], target),
        )

    def receive(j, h, u):
        for copy in sends(j, h, u):
            copy.wait_recv()
        return decode(rq[j, h, u], rs[j, h, u])

    def pass_on(j, h, u, came):
        v = part[(h * 2 + u) * SUB : (h * 2 + u + 1) * SUB]
        if came:
            v = v + receive(j - 1, h, u)
        code, scale = encode(v)
        sq[j, h, u] = code
        ss[j, h, u] = scale
        for copy in sends(j, h, u):
            copy.start()

    hand(0)
    start2(2)
    arrived(0)
    right(0)
    part[0:ROWS] = product(0)
    for u in range(2):
        pass_on(0, 0, u, False)

    for j in (1, 2, 3):
        hand(j)
        if j < 3:
            start2(j + 2)
        arrived(j)
        right(j)
        for h in (1, 0):
            part[h * ROWS : (h + 1) * ROWS] = product(h)
        for h in (1, 0):
            for u in range(2):
                pass_on(j, h, u, j > 1 or h == 0)

    hand(4)
    arrived(4)
    right(4)
    own_part[...] = product(0)
    for u in range(2):
        rows = slice(u * SUB, (u + 1) * SUB)
        v = own_part[rows]
        for c in range(2):
            for ref, sem in ((fq, rfq), (fs, rfs)):
                remote(ref.at[c, u], ref.at[c, u], szq.at[3, 0, u], sem.at[c, u], at(step, 0, 0, core)).wait_recv()
            v = v + decode(fq[c, u], fs[c, u])
        out[rows] = v

    lam_copy.wait_send()
    for g in range(5):
        for t in (1, 2, 3):
            phase1(g, t).wait_send()
            phase2(g, t).wait_send()
        for t in range(4):
            handing(g, t).wait_send()
    for j in range(4):
        for h in range(2):
            for u in range(2):
                if j > 0 or h == 0:
                    for copy in sends(j, h, u):
                        copy.wait_send()


def per_device(lambda_amp, lambda_tiles, integrals, integral_tiles):
    dma = pltpu.SemaphoreType.DMA
    hbm = pl.BlockSpec(memory_space=pl.ANY)
    return pl.pallas_call(
        kernel,
        out_shape=jax.ShapeDtypeStruct((ROWS, W), F32),
        in_specs=[hbm, hbm, hbm, pl.BlockSpec(memory_space=pltpu.SMEM)],
        out_specs=pl.BlockSpec(memory_space=pltpu.VMEM),
        scratch_shapes=[
            pltpu.VMEM((ROWS, W), F32),
            pltpu.VMEM((ROWS, 3), I32),
            pltpu.VMEM((12, 8 * W), F32),
            pltpu.VMEM((ROWS, W), F32),
            pltpu.VMEM((2, 4, 4, 2, 8, W), F32),
            pltpu.VMEM((2, 4, 4, 2, 8, W), F32),
            pltpu.VMEM((3, 4, 4, 3, 8, W), F32),
            pltpu.VMEM((3, 4, 4, 2, 8, W), F32),
            pltpu.VMEM((2 * ROWS, 4 * W), BF16),
            pltpu.VMEM((2 * ROWS, 2 * W), BF16),
            pltpu.VMEM((4 * W, W), BF16),
            pltpu.VMEM((2 * ROWS, W), F32),
            pltpu.VMEM((ROWS, W), F32),
            pltpu.VMEM((4, 2, 2, SUB, W), I16),
            pltpu.VMEM((4, 2, 2, 1, W), F32),
            pltpu.VMEM((3, 2, 2, SUB, W), I16),
            pltpu.VMEM((3, 2, 2, 1, W), F32),
            pltpu.VMEM((2, 2, SUB, W), I16),
            pltpu.VMEM((2, 2, 1, W), F32),
            dma((3,)),
            dma((5, 3)),
            dma((5, 3)),
            dma((5, 3)),
            dma((5, 3)),
            dma((5, 4)),
            dma((5, 4)),
            dma,
            dma,
            dma((4, 2, 2)),
            dma((4, 2, 2)),
            dma((3, 2, 2)),
            dma((3, 2, 2)),
            dma((2, 2)),
            dma((2, 2)),
        ],
        compiler_params=pltpu.CompilerParams(
            collective_id=0, has_side_effects=True, vmem_limit_bytes=48 << 20
        ),
        cost_estimate=pl.CostEstimate(flops=3_700_000_000, bytes_accessed=1_500_000, transcendentals=0),
    )(lambda_amp, lambda_tiles, integrals, integral_tiles)


def solution(mesh):
    placed = (P("own", "rep"), P("own", "rep"), P(("rep", "own"), None), P())
    return jax.shard_map(
        per_device, mesh=mesh, in_specs=placed, out_specs=P("own", "rep"), check_vma=False
    )
```

```python
import jax
import jax.numpy as jnp
from jax import lax
from jax.experimental import pallas as pl
from jax.experimental.pallas import tpu as pltpu
from jax.sharding import PartitionSpec as P

MESH = pl.DeviceIdType.MESH
F32, BF16, I32, I16 = jnp.float32, jnp.bfloat16, jnp.int32, jnp.int16
TILE = 128
W = 384
ROWS = 256
SUB = 128
Q = 32767.0


def split3(v):
    first = v.astype(BF16)
    rest = v - first.astype(F32)
    second = rest.astype(BF16)
    rest = rest - second.astype(F32)
    return first, second, rest.astype(BF16)


def encode(v):
    top = jnp.maximum(jnp.max(jnp.abs(v), axis=0, keepdims=True), 1e-30)
    code = jnp.round(v * (Q / top)).astype(I32).astype(I16)
    return code, top * (1.0 / Q)


def decode(code, scale):
    return code.astype(I32).astype(F32) * scale


def kernel(
    lam_hbm, keep_hbm, ints_hbm, flags_hbm, out_hbm,
    lam, keep, ints, flags, lamx, came, relay, gath, la, lb, ra, part, result, total,
    sq, ss, rq, rs, fq, fs,
    in_sem, out_sem, s1, r1, s2, r2, sl, rl, so, ro, szq, szs, rzq, rzs, rfq, rfs,
):
    z = lax.axis_index("rep")
    own = lax.axis_index("own")
    core = lax.rem(own, 2)
    x = own // 8
    y = lax.rem(own // 2, 4)
    a = x + core * (y - x)
    b = y + core * (x - y)
    step = 1 - 2 * core

    def at(dz, da, db, c):
        aa, bb = lax.rem(a + da, 4), lax.rem(b + db, 4)
        xx, yy = aa + core * (bb - aa), bb + core * (aa - bb)
        return (lax.rem(z + dz + 8, 8), (xx * 4 + yy) * 2 + c)

    def chunk(distance, c):
        return lax.rem(z + distance * (1 - 2 * c) + 8, 8)

    def remote(src, dst, send, recv, device):
        return pltpu.make_async_remote_copy(
            src_ref=src, dst_ref=dst, send_sem=send, recv_sem=recv, device_id=device, device_id_type=MESH
        )

    barrier = pltpu.get_barrier_semaphore()
    peers = [at(0, t, 0, 1 - core) for t in range(4)] + [at(0, 0, t, 1 - core) for t in (1, 2, 3)]
    peers += [at(0, t, 0, core) for t in (1, 2, 3)] + [at(0, 0, t, core) for t in (1, 2, 3)]
    peers += [at(d, 0, 0, c) for d in (1, -1) for c in (core, 1 - core)]
    for peer in peers:
        pl.semaphore_signal(barrier, inc=1, device_id=peer, device_id_type=MESH)

    loads = [
        pltpu.make_async_copy(ints_hbm, ints, in_sem.at[0]),
        pltpu.make_async_copy(flags_hbm, flags, in_sem.at[1]),
        pltpu.make_async_copy(lam_hbm, lam, in_sem.at[2]),
        pltpu.make_async_copy(keep_hbm, keep, in_sem.at[3]),
    ]
    for load in loads:
        load.start()
    loads[0].wait()
    loads[1].wait()

    first_row = own * 12
    t0 = first_row // TILE
    t1 = (first_row + 11) // TILE
    bound = (t0 + 1) * TILE - first_row
    above = lax.broadcasted_iota(I32, (12, TILE), 0) < bound
    odd = lax.rem(b, 2)

    def masked(ch, u):
        cols = pl.ds(pl.multiple_of(ch * W + u * TILE, TILE), TILE)
        f0 = flags[3 * z + t0, 3 * ch + u].astype(F32)
        f1 = flags[3 * z + t1, 3 * ch + u].astype(F32)
        return ints[:, cols] * jnp.where(above, f0, f1)

    def pack(g):
        for u in range(3):
            to = slice(u * TILE, (u + 1) * TILE)
            if g in (0, 4):
                v = masked(chunk(4 - g, 0), u)
                came[g, b, 1, :, to] = v[0:8]
                came[g, b, 2, 0:4, to] = v[8:12]
                came[g, b, 2, 4:8, to] = v[8:12]
            else:
                v = masked(chunk(4 - g, odd), u)
                came[g, b, odd, :, to] = v[0:8]
                came[g, b, 2, 0:4, to] = v[8:12]
                v = masked(chunk(4 - g, 1 - odd), u)
                came[g, b, 1 - odd, :, to] = v[0:8]
                came[g, b, 2, 4:8, to] = v[8:12]

    for g in range(5):
        pack(g)

    def phase1(g, t, slot):
        rows = came.at[g, slot, pl.ds(1, 2)] if g in (0, 4) else came.at[g, slot]
        return remote(rows, rows, s1.at[g, t - 1], r1.at[g, slot], at(0, 0, t, core))

    def start1(g):
        for t in (1, 3, 2):
            phase1(g, t, b).start()

    def phase2(g, o, t):
        src = gath.at[g, core, a] if o == 0 else relay.at[g]
        return remote(src, gath.at[g, core, a], s2.at[g, o, t], r2.at[g, core, a], at(0, t, 0, core + o - 2 * core * o))

    def phase2_came(g, o, t):
        c, slot = (core, lax.rem(a + t, 4)) if o == 0 else (1 - core, lax.rem(b + t, 4))
        device = at(0, t, 0, c) if o == 0 else at(0, 0, t, c)
        return remote(gath.at[g, c, slot], gath.at[g, c, slot], s2.at[g, o, t], r2.at[g, c, slot], device)

    same, other = ((0, 1), (0, 3), (0, 2)), ((1, 1), (1, 3), (1, 2), (1, 0))
    low = lax.broadcasted_iota(I32, (8, W), 0) < 4
    mine_first = (lax.broadcasted_iota(I32, (8, W), 0) < 4) == (core == 0)

    def split_by_core(g, ours, theirs):
        pl.when(core == g // 4)(ours)
        pl.when(core != g // 4)(theirs)

    def start2(g):
        for t in (1, 3, 2):
            phase1(g, t, lax.rem(b + t, 4)).wait_recv()
        for i in range(4):
            gath[g, core, a, i] = came[g, i, 1 if g in (0, 4) else core]
            relay[g, i] = came[g, i, 1 if g in (0, 4) else 1 - core]
        for i in range(2):
            even, uneven = came[g, 2 * i, 2], came[g, 2 * i + 1, 2]
            if g in (0, 4):
                tail = jnp.where(low, even, uneven) if g == 0 else jnp.where(low, uneven, even)
                gath[g, core, a, 4 + i] = tail
                relay[g, 4 + i] = tail
            else:
                gath[g, core, a, 4 + i] = jnp.where(mine_first, even, uneven)
                relay[g, 4 + i] = jnp.where(mine_first, uneven, even)
        if g in (0, 4):
            split_by_core(
                g,
                lambda: [phase2(g, o, t).start() for o, t in same] and None,
                lambda: [phase2(g, o, t).start() for o, t in other] and None,
            )
        else:
            for o, t in same + other:
                phase2(g, o, t).start()

    def arrived(g):
        for o, t in same + other:
            phase2_came(g, o, t).wait_recv()

    lam_copy = remote(lam, lamx, sl, rl, at(0, 0, 0, 1 - core))

    pl.semaphore_wait(barrier, len(peers))
    start1(0)
    start1(1)

    loads[2].wait()
    loads[3].wait()
    kept = jnp.concatenate([keep[...].astype(F32), jnp.zeros((5, ROWS), F32)], axis=0).T
    for u in range(3):
        cols = slice(u * TILE, (u + 1) * TILE)
        lam[:, cols] = lam[:, cols] * kept[:, u : u + 1]
    lam_copy.start()
    start1(2)
    start1(3)
    start1(4)

    n = lax.broadcasted_iota(I32, (1, W), 1)
    origin = (n >= 192).astype(I32)
    n = n - 192 * origin
    ia = (n * 1366) >> 16
    n = n - 48 * ia
    tile, r = n >> 3, n & 7
    half = r >> 2
    ib = jnp.where(tile < 4, tile, 2 * (tile - 4) + half + core - 2 * core * half)
    chip = jnp.where(origin == 0, ia * 4 + ib, ib * 4 + ia)
    place = 24 * chip + 12 * origin + jnp.where(tile < 4, r, 8 + (r & 3))
    order = (lax.broadcasted_iota(I32, (W, W), 0) == place).astype(BF16)

    def prepare(values, h):
        rows = slice(h * ROWS, (h + 1) * ROWS)
        l1, l2, l3 = (jnp.dot(s, order, preferred_element_type=F32).astype(BF16) for s in split3(values))
        for i, s in enumerate((l1, l1, l1, l3)):
            la[rows, i * W : (i + 1) * W] = s
        for i in range(2):
            lb[rows, i * W : (i + 1) * W] = l2

    prepare(lam[...], 0)
    for g in range(4):
        start2(g)
    lam_copy.wait_recv()
    prepare(lamx[...], 1)

    def right(g):
        for i in range(8):
            r1_, r2_, r3_ = split3(gath[g, i // 4, i % 4].reshape(48, W))
            for k, s in enumerate((r1_, r2_, r3_, r1_)):
                ra[k * W + i * 48 : k * W + (i + 1) * 48] = s

    def product(h):
        rows = slice(h * ROWS, (h + 1) * ROWS)
        most = jnp.dot(la[rows], ra[...], preferred_element_type=F32)
        return most + jnp.dot(lb[rows], ra[0 : 2 * W], preferred_element_type=F32)

    def sends(j, h, u):
        if j < 3:
            target = at(step, 0, 0, core) if j else at(1 - 2 * h, 0, 0, h)
            hh = h if j else 0
            to = (rq.at[j, hh, u], rs.at[j, hh, u], rzq.at[j, hh, u], rzs.at[j, hh, u])
        else:
            target = at(step, 0, 0, core if h == 0 else 1 - core)
            to = (fq.at[core, u], fs.at[core, u], rfq.at[core, u], rfs.at[core, u])
        return (
            remote(sq.at[j, h, u], to[0], szq.at[j, h, u], to[2], target),
            remote(ss.at[j, h, u], to[1], szs.at[j, h, u], to[3], target),
        )

    def came_in(q_ref, s_ref, q_sem, s_sem):
        for ref, sem in ((q_ref, q_sem), (s_ref, s_sem)):
            remote(ref, ref, szq.at[3, 0, 0], sem, at(step, 0, 0, core)).wait_recv()
        return decode(q_ref[...], s_ref[...])

    def pass_on(j, h, u, add):
        v = part[(h * 2 + u) * SUB : (h * 2 + u + 1) * SUB]
        if add:
            at_ = (j - 1, h, u)
            v = v + came_in(rq.at[at_], rs.at[at_], rzq.at[at_], rzs.at[at_])
        code, scale = encode(v)
        sq[j, h, u] = code
        ss[j, h, u] = scale
        for copy in sends(j, h, u):
            copy.start()

    own_copy = remote(part.at[pl.ds(ROWS, ROWS)], result, so, ro, at(0, 0, 0, 1 - core))

    @pl.when(core == 0)
    def _():
        arrived(0)
        right(0)
        for h in (1, 0):
            part[h * ROWS : (h + 1) * ROWS] = product(h)
            for u in range(2):
                pass_on(0, h, u, False)

    start2(4)

    for j in (1, 2, 3):
        arrived(j)
        right(j)
        for h in (1, 0):
            part[h * ROWS : (h + 1) * ROWS] = product(h)
            if j == 1:
                for u in range(2):
                    pass_on(j, h, u, h == 0)
        if j > 1:
            for h in (1, 0):
                for u in range(2):
                    pass_on(j, h, u, True)

    @pl.when(core == 1)
    def _():
        arrived(4)
        right(4)
        part[ROWS : 2 * ROWS] = product(1)
        own_copy.start()
        result[...] = product(0)

    @pl.when(core == 0)
    def _():
        own_copy.wait_recv()

    stores = []
    for u in range(2):
        rows = slice(u * SUB, (u + 1) * SUB)
        v = result[rows]
        for c in range(2):
            at_ = (c, u)
            v = v + came_in(fq.at[at_], fs.at[at_], rfq.at[at_], rfs.at[at_])
        total[rows] = v
        stores.append(pltpu.make_async_copy(total.at[rows], out_hbm.at[rows], out_sem.at[u]))
        stores[u].start()

    lam_copy.wait_send()
    for g in range(5):
        for t in (1, 2, 3):
            phase1(g, t, b).wait_send()
        if g in (0, 4):
            split_by_core(
                g,
                lambda: [phase2(g, o, t).wait_send() for o, t in same] and None,
                lambda: [phase2(g, o, t).wait_send() for o, t in other] and None,
            )
        else:
            for o, t in same + other:
                phase2(g, o, t).wait_send()

    @pl.when(core == 0)
    def _():
        for h in range(2):
            for u in range(2):
                for copy in sends(0, h, u):
                    copy.wait_send()

    @pl.when(core == 1)
    def _():
        own_copy.wait_send()

    for j in (1, 2, 3):
        for h in range(2):
            for u in range(2):
                for copy in sends(j, h, u):
                    copy.wait_send()
    for store in stores:
        store.wait()


def per_device(lambda_amp, lambda_tiles, integrals, integral_tiles):
    dma = pltpu.SemaphoreType.DMA
    hbm = pl.BlockSpec(memory_space=pl.ANY)
    return pl.pallas_call(
        kernel,
        out_shape=jax.ShapeDtypeStruct((ROWS, W), F32),
        in_specs=[hbm] * 4,
        out_specs=hbm,
        scratch_shapes=[
            pltpu.VMEM((ROWS, W), F32),
            pltpu.VMEM((3, ROWS), I32),
            pltpu.VMEM((12, 8 * W), F32),
            pltpu.SMEM((24, 24), I32),
            pltpu.VMEM((ROWS, W), F32),
            pltpu.VMEM((5, 4, 3, 8, W), F32),
            pltpu.VMEM((5, 6, 8, W), F32),
            pltpu.VMEM((5, 2, 4, 6, 8, W), F32),
            pltpu.VMEM((2 * ROWS, 4 * W), BF16),
            pltpu.VMEM((2 * ROWS, 2 * W), BF16),
            pltpu.VMEM((4 * W, W), BF16),
            pltpu.VMEM((2 * ROWS, W), F32),
            pltpu.VMEM((ROWS, W), F32),
            pltpu.VMEM((ROWS, W), F32),
            pltpu.VMEM((4, 2, 2, SUB, W), I16),
            pltpu.VMEM((4, 2, 2, 1, W), F32),
            pltpu.VMEM((3, 2, 2, SUB, W), I16),
            pltpu.VMEM((3, 2, 2, 1, W), F32),
            pltpu.VMEM((2, 2, SUB, W), I16),
            pltpu.VMEM((2, 2, 1, W), F32),
            dma((4,)),
            dma((2,)),
            dma((5, 3)),
            dma((5, 4)),
            dma((5, 2, 4)),
            dma((5, 2, 4)),
            dma,
            dma,
            dma,
            dma,
            dma((4, 2, 2)),
            dma((4, 2, 2)),
            dma((3, 2, 2)),
            dma((3, 2, 2)),
            dma((2, 2)),
            dma((2, 2)),
        ],
        compiler_params=pltpu.CompilerParams(
            collective_id=0, has_side_effects=True, vmem_limit_bytes=60 << 20
        ),
        cost_estimate=pl.CostEstimate(flops=3_700_000_000, bytes_accessed=1_500_000, transcendentals=0),
    )(lambda_amp, lambda_tiles.T, integrals, integral_tiles)


def solution(mesh):
    placed = (P("own", "rep"), P("own", "rep"), P(("rep", "own"), None), P())
    return jax.shard_map(
        per_device, mesh=mesh, in_specs=placed, out_specs=P("own", "rep"), check_vma=False
    )
```

```python
import jax
import jax.numpy as jnp
from jax import lax
from jax.experimental import pallas as pl
from jax.experimental.pallas import tpu as pltpu
from jax.sharding import PartitionSpec as P

MESH = pl.DeviceIdType.MESH
F32, BF16, I32, I16 = jnp.float32, jnp.bfloat16, jnp.int32, jnp.int16
TILE = 128
W = 384
ROWS = 256
SUB = 128
Q = 32767.0


def split3(v):
    first = v.astype(BF16)
    rest = v - first.astype(F32)
    second = rest.astype(BF16)
    rest = rest - second.astype(F32)
    return first, second, rest.astype(BF16)


def encode(v):
    top = jnp.maximum(jnp.max(jnp.abs(v), axis=0, keepdims=True), 1e-30)
    code = jnp.round(v * (Q / top)).astype(I32).astype(I16)
    return code, top * (1.0 / Q)


def decode(code, scale):
    return code.astype(I32).astype(F32) * scale


def kernel(
    lam_hbm, keep_hbm, ints_hbm, flags_hbm, out_hbm,
    lam, keep, ints, flags, lamx, came, relay, gath, la, lb, ra, part, result, total,
    sq, ss, rq, rs, fq, fs,
    in_sem, out_sem, s1, r1, s2, r2, sl, rl, so, ro, szq, szs, rzq, rzs, rfq, rfs,
):
    z = lax.axis_index("rep")
    own = lax.axis_index("own")
    core = lax.rem(own, 2)
    x = own // 8
    y = lax.rem(own // 2, 4)
    a = x + core * (y - x)
    b = y + core * (x - y)
    step = 1 - 2 * core

    def at(dz, da, db, c):
        aa, bb = lax.rem(a + da, 4), lax.rem(b + db, 4)
        xx, yy = aa + core * (bb - aa), bb + core * (aa - bb)
        return (lax.rem(z + dz + 8, 8), (xx * 4 + yy) * 2 + c)

    def chunk(distance, c):
        return lax.rem(z + distance * (1 - 2 * c) + 8, 8)

    def remote(src, dst, send, recv, device):
        return pltpu.make_async_remote_copy(
            src_ref=src, dst_ref=dst, send_sem=send, recv_sem=recv, device_id=device, device_id_type=MESH
        )

    barrier = pltpu.get_barrier_semaphore()
    peers = [at(0, t, 0, 1 - core) for t in range(4)] + [at(0, 0, t, 1 - core) for t in (1, 2, 3)]
    peers += [at(0, t, 0, core) for t in (1, 2, 3)] + [at(0, 0, t, core) for t in (1, 2, 3)]
    peers += [at(d, 0, 0, c) for d in (1, -1) for c in (core, 1 - core)]
    for peer in peers:
        pl.semaphore_signal(barrier, inc=1, device_id=peer, device_id_type=MESH)

    loads = [
        pltpu.make_async_copy(ints_hbm, ints, in_sem.at[0]),
        pltpu.make_async_copy(flags_hbm, flags, in_sem.at[1]),
        pltpu.make_async_copy(lam_hbm, lam, in_sem.at[2]),
        pltpu.make_async_copy(keep_hbm, keep, in_sem.at[3]),
    ]
    for load in loads:
        load.start()
    loads[0].wait()
    loads[1].wait()

    first_row = own * 12
    t0 = first_row // TILE
    t1 = (first_row + 11) // TILE
    bound = (t0 + 1) * TILE - first_row
    above = lax.broadcasted_iota(I32, (12, TILE), 0) < bound
    odd = lax.rem(b, 2)

    def masked(ch, u):
        cols = pl.ds(pl.multiple_of(ch * W + u * TILE, TILE), TILE)
        f0 = flags[3 * z + t0, 3 * ch + u].astype(F32)
        f1 = flags[3 * z + t1, 3 * ch + u].astype(F32)
        return ints[:, cols] * jnp.where(above, f0, f1)

    def pack(g):
        for u in range(3):
            to = slice(u * TILE, (u + 1) * TILE)
            if g in (0, 4):
                v = masked(chunk(4 - g, 0), u)
                came[g, b, 1, :, to] = v[0:8]
                came[g, b, 2, 0:4, to] = v[8:12]
                came[g, b, 2, 4:8, to] = v[8:12]
            else:
                v = masked(chunk(4 - g, odd), u)
                came[g, b, odd, :, to] = v[0:8]
                came[g, b, 2, 0:4, to] = v[8:12]
                v = masked(chunk(4 - g, 1 - odd), u)
                came[g, b, 1 - odd, :, to] = v[0:8]
                came[g, b, 2, 4:8, to] = v[8:12]

    for g in range(5):
        pack(g)

    def phase1(g, t, slot):
        rows = came.at[g, slot, pl.ds(1, 2)] if g in (0, 4) else came.at[g, slot]
        return remote(rows, rows, s1.at[g, t - 1], r1.at[g, slot], at(0, 0, t, core))

    def start1(g):
        for t in (1, 3, 2):
            phase1(g, t, b).start()

    def phase2(g, o, t):
        src = gath.at[g, core, a] if o == 0 else relay.at[g]
        return remote(src, gath.at[g, core, a], s2.at[g, o, t], r2.at[g, core, a], at(0, t, 0, core + o - 2 * core * o))

    def phase2_came(g, o, t):
        c, slot = (core, lax.rem(a + t, 4)) if o == 0 else (1 - core, lax.rem(b + t, 4))
        device = at(0, t, 0, c) if o == 0 else at(0, 0, t, c)
        return remote(gath.at[g, c, slot], gath.at[g, c, slot], s2.at[g, o, t], r2.at[g, c, slot], device)

    same, other = ((0, 1), (0, 3), (0, 2)), ((1, 1), (1, 3), (1, 2), (1, 0))
    low = lax.broadcasted_iota(I32, (8, W), 0) < 4
    mine_first = (lax.broadcasted_iota(I32, (8, W), 0) < 4) == (core == 0)

    def split_by_core(g, ours, theirs):
        pl.when(core == g // 4)(ours)
        pl.when(core != g // 4)(theirs)

    def start2(g):
        for t in (1, 3, 2):
            phase1(g, t, lax.rem(b + t, 4)).wait_recv()
        for i in range(4):
            gath[g, core, a, i] = came[g, i, 1 if g in (0, 4) else core]
            relay[g, i] = came[g, i, 1 if g in (0, 4) else 1 - core]
        for i in range(2):
            even, uneven = came[g, 2 * i, 2], came[g, 2 * i + 1, 2]
            if g in (0, 4):
                tail = jnp.where(low, even, uneven) if g == 0 else jnp.where(low, uneven, even)
                gath[g, core, a, 4 + i] = tail
                relay[g, 4 + i] = tail
            else:
                gath[g, core, a, 4 + i] = jnp.where(mine_first, even, uneven)
                relay[g, 4 + i] = jnp.where(mine_first, uneven, even)
        if g in (0, 4):
            split_by_core(
                g,
                lambda: [phase2(g, o, t).start() for o, t in same] and None,
                lambda: [phase2(g, o, t).start() for o, t in other] and None,
            )
        else:
            for o, t in same + other:
                phase2(g, o, t).start()

    def arrived(g):
        for o, t in same + other:
            phase2_came(g, o, t).wait_recv()

    lam_copy = remote(lam, lamx, sl, rl, at(0, 0, 0, 1 - core))

    pl.semaphore_wait(barrier, len(peers))
    start1(0)
    start1(1)

    loads[2].wait()
    loads[3].wait()
    kept = jnp.concatenate([keep[...].astype(F32), jnp.zeros((5, ROWS), F32)], axis=0).T
    for u in range(3):
        cols = slice(u * TILE, (u + 1) * TILE)
        lam[:, cols] = lam[:, cols] * kept[:, u : u + 1]
    lam_copy.start()
    start1(2)
    start1(3)
    start1(4)

    n = lax.broadcasted_iota(I32, (1, W), 1)
    origin = (n >= 192).astype(I32)
    n = n - 192 * origin
    ia = (n * 1366) >> 16
    n = n - 48 * ia
    tile, r = n >> 3, n & 7
    half = r >> 2
    ib = jnp.where(tile < 4, tile, 2 * (tile - 4) + half + core - 2 * core * half)
    chip = jnp.where(origin == 0, ia * 4 + ib, ib * 4 + ia)
    place = 24 * chip + 12 * origin + jnp.where(tile < 4, r, 8 + (r & 3))
    order = (lax.broadcasted_iota(I32, (W, W), 0) == place).astype(BF16)

    def prepare(values, h):
        rows = slice(h * ROWS, (h + 1) * ROWS)
        l1, l2, l3 = (jnp.dot(s, order, preferred_element_type=F32).astype(BF16) for s in split3(values))
        for i, s in enumerate((l1, l1, l1, l3)):
            la[rows, i * W : (i + 1) * W] = s
        for i in range(2):
            lb[rows, i * W : (i + 1) * W] = l2

    prepare(lam[...], 0)
    for g in range(4):
        start2(g)
    lam_copy.wait_recv()
    prepare(lamx[...], 1)

    def right(g):
        for i in range(8):
            r1_, r2_, r3_ = split3(gath[g, i // 4, i % 4].reshape(48, W))
            for k, s in enumerate((r1_, r2_, r3_, r1_)):
                ra[k * W + i * 48 : k * W + (i + 1) * 48] = s

    def product(h):
        rows = slice(h * ROWS, (h + 1) * ROWS)
        most = jnp.dot(la[rows], ra[...], preferred_element_type=F32)
        return most + jnp.dot(lb[rows], ra[0 : 2 * W], preferred_element_type=F32)

    def sends(j, h, u):
        if j < 3:
            target = at(step, 0, 0, core) if j else at(1 - 2 * h, 0, 0, h)
            hh = h if j else 0
            to = (rq.at[j, hh, u], rs.at[j, hh, u], rzq.at[j, hh, u], rzs.at[j, hh, u])
        else:
            target = at(step, 0, 0, core if h == 0 else 1 - core)
            to = (fq.at[core, u], fs.at[core, u], rfq.at[core, u], rfs.at[core, u])
        return (
            remote(sq.at[j, h, u], to[0], szq.at[j, h, u], to[2], target),
            remote(ss.at[j, h, u], to[1], szs.at[j, h, u], to[3], target),
        )

    def came_in(q_ref, s_ref, q_sem, s_sem):
        for ref, sem in ((q_ref, q_sem), (s_ref, s_sem)):
            remote(ref, ref, szq.at[3, 0, 0], sem, at(step, 0, 0, core)).wait_recv()
        return decode(q_ref[...], s_ref[...])

    def pass_on(j, h, u, add):
        v = part[(h * 2 + u) * SUB : (h * 2 + u + 1) * SUB]
        if add:
            at_ = (j - 1, h, u)
            v = v + came_in(rq.at[at_], rs.at[at_], rzq.at[at_], rzs.at[at_])
        code, scale = encode(v)
        sq[j, h, u] = code
        ss[j, h, u] = scale
        for copy in sends(j, h, u):
            copy.start()

    own_copy = remote(part.at[pl.ds(ROWS, ROWS)], result, so, ro, at(0, 0, 0, 1 - core))

    @pl.when(core == 0)
    def _():
        arrived(0)
        right(0)
        for h in (1, 0):
            part[h * ROWS : (h + 1) * ROWS] = product(h)
            for u in range(2):
                pass_on(0, h, u, False)

    start2(4)

    for j in (1, 2, 3):
        arrived(j)
        right(j)
        for h in (1, 0):
            part[h * ROWS : (h + 1) * ROWS] = product(h)
            for u in range(2):
                pass_on(j, h, u, j > 1 or h == 0)

    @pl.when(core == 1)
    def _():
        arrived(4)
        right(4)
        part[ROWS : 2 * ROWS] = product(1)
        own_copy.start()
        result[...] = product(0)

    @pl.when(core == 0)
    def _():
        own_copy.wait_recv()

    for u in range(2):
        rows = slice(u * SUB, (u + 1) * SUB)
        v = result[rows]
        for c in range(2):
            at_ = (c, u)
            v = v + came_in(fq.at[at_], fs.at[at_], rfq.at[at_], rfs.at[at_])
        out_hbm[rows] = v

    lam_copy.wait_send()
    for g in range(5):
        for t in (1, 2, 3):
            phase1(g, t, b).wait_send()
        if g in (0, 4):
            split_by_core(
                g,
                lambda: [phase2(g, o, t).wait_send() for o, t in same] and None,
                lambda: [phase2(g, o, t).wait_send() for o, t in other] and None,
            )
        else:
            for o, t in same + other:
                phase2(g, o, t).wait_send()

    @pl.when(core == 0)
    def _():
        for h in range(2):
            for u in range(2):
                for copy in sends(0, h, u):
                    copy.wait_send()

    @pl.when(core == 1)
    def _():
        own_copy.wait_send()

    for j in (1, 2, 3):
        for h in range(2):
            for u in range(2):
                for copy in sends(j, h, u):
                    copy.wait_send()


def per_device(lambda_amp, lambda_tiles, integrals, integral_tiles):
    dma = pltpu.SemaphoreType.DMA
    hbm = pl.BlockSpec(memory_space=pl.ANY)
    return pl.pallas_call(
        kernel,
        out_shape=pltpu.VMEM((ROWS, W), F32),
        in_specs=[hbm] * 4,
        out_specs=pl.BlockSpec(memory_space=pltpu.VMEM),
        scratch_shapes=[
            pltpu.VMEM((ROWS, W), F32),
            pltpu.VMEM((3, ROWS), I32),
            pltpu.VMEM((12, 8 * W), F32),
            pltpu.SMEM((24, 24), I32),
            pltpu.VMEM((ROWS, W), F32),
            pltpu.VMEM((5, 4, 3, 8, W), F32),
            pltpu.VMEM((5, 6, 8, W), F32),
            pltpu.VMEM((5, 2, 4, 6, 8, W), F32),
            pltpu.VMEM((2 * ROWS, 4 * W), BF16),
            pltpu.VMEM((2 * ROWS, 2 * W), BF16),
            pltpu.VMEM((4 * W, W), BF16),
            pltpu.VMEM((2 * ROWS, W), F32),
            pltpu.VMEM((ROWS, W), F32),
            pltpu.VMEM((ROWS, W), F32),
            pltpu.VMEM((4, 2, 2, SUB, W), I16),
            pltpu.VMEM((4, 2, 2, 1, W), F32),
            pltpu.VMEM((3, 2, 2, SUB, W), I16),
            pltpu.VMEM((3, 2, 2, 1, W), F32),
            pltpu.VMEM((2, 2, SUB, W), I16),
            pltpu.VMEM((2, 2, 1, W), F32),
            dma((4,)),
            dma((2,)),
            dma((5, 3)),
            dma((5, 4)),
            dma((5, 2, 4)),
            dma((5, 2, 4)),
            dma,
            dma,
            dma,
            dma,
            dma((4, 2, 2)),
            dma((4, 2, 2)),
            dma((3, 2, 2)),
            dma((3, 2, 2)),
            dma((2, 2)),
            dma((2, 2)),
        ],
        compiler_params=pltpu.CompilerParams(
            collective_id=0, has_side_effects=True, vmem_limit_bytes=48 << 20
        ),
        cost_estimate=pl.CostEstimate(flops=3_700_000_000, bytes_accessed=1_500_000, transcendentals=0),
    )(*(pltpu.with_memory_space_constraint(v, pltpu.HBM) for v in (lambda_amp, lambda_tiles.T, integrals, integral_tiles)))


def solution(mesh):
    placed = (P("own", "rep"), P("own", "rep"), P(("rep", "own"), None), P())
    return jax.shard_map(
        per_device, mesh=mesh, in_specs=placed, out_specs=P("own", "rep"), check_vma=False
    )
```

```python
import jax
import jax.numpy as jnp
from jax import lax
from jax.experimental import pallas as pl
from jax.experimental.pallas import tpu as pltpu
from jax.sharding import PartitionSpec as P

MESH = pl.DeviceIdType.MESH
F32, BF16, I32, I16 = jnp.float32, jnp.bfloat16, jnp.int32, jnp.int16
TILE = 128
W = 384
ROWS = 256
SUB = 128
Q = 32767.0


def split3(v):
    first = v.astype(BF16)
    rest = v - first.astype(F32)
    second = rest.astype(BF16)
    rest = rest - second.astype(F32)
    return first, second, rest.astype(BF16)


def encode(v):
    top = jnp.maximum(jnp.max(jnp.abs(v), axis=0, keepdims=True), 1e-30)
    code = jnp.round(v * (Q / top)).astype(I32).astype(I16)
    return code, top * (1.0 / Q)


def decode(code, scale):
    return code.astype(I32).astype(F32) * scale


def kernel(
    lam_hbm, keep_hbm, ints_hbm, flags_hbm, out_hbm,
    lam, keep, ints, flags, lamx, came, relay, gath, la, lb, ra, part, result, total,
    sq, ss, rq, rs, fq, fs,
    in_sem, out_sem, s1, r1, s2, r2, sl, rl, so, ro, szq, szs, rzq, rzs, rfq, rfs,
):
    z = lax.axis_index("rep")
    own = lax.axis_index("own")
    core = lax.rem(own, 2)
    x = own // 8
    y = lax.rem(own // 2, 4)
    a = x + core * (y - x)
    b = y + core * (x - y)
    step = 1 - 2 * core

    def at(dz, da, db, c):
        aa, bb = lax.rem(a + da, 4), lax.rem(b + db, 4)
        xx, yy = aa + core * (bb - aa), bb + core * (aa - bb)
        return (lax.rem(z + dz + 8, 8), (xx * 4 + yy) * 2 + c)

    def chunk(distance, c):
        return lax.rem(z + distance * (1 - 2 * c) + 8, 8)

    def remote(src, dst, send, recv, device):
        return pltpu.make_async_remote_copy(
            src_ref=src, dst_ref=dst, send_sem=send, recv_sem=recv, device_id=device, device_id_type=MESH
        )

    barrier = pltpu.get_barrier_semaphore()
    peers = [at(0, t, 0, 1 - core) for t in range(4)] + [at(0, 0, t, 1 - core) for t in (1, 2, 3)]
    peers += [at(0, t, 0, core) for t in (1, 2, 3)] + [at(0, 0, t, core) for t in (1, 2, 3)]
    peers += [at(d, 0, 0, c) for d in (1, -1) for c in (core, 1 - core)]
    for peer in peers:
        pl.semaphore_signal(barrier, inc=1, device_id=peer, device_id_type=MESH)

    loads = [
        pltpu.make_async_copy(ints_hbm, ints, in_sem.at[0]),
        pltpu.make_async_copy(flags_hbm, flags, in_sem.at[1]),
        pltpu.make_async_copy(lam_hbm, lam, in_sem.at[2]),
        pltpu.make_async_copy(keep_hbm, keep, in_sem.at[3]),
    ]
    for load in loads:
        load.start()
    loads[0].wait()
    loads[1].wait()

    first_row = own * 12
    t0 = first_row // TILE
    t1 = (first_row + 11) // TILE
    bound = (t0 + 1) * TILE - first_row
    above = lax.broadcasted_iota(I32, (12, TILE), 0) < bound
    odd = lax.rem(b, 2)

    def masked(ch, u):
        cols = pl.ds(pl.multiple_of(ch * W + u * TILE, TILE), TILE)
        f0 = flags[3 * z + t0, 3 * ch + u].astype(F32)
        f1 = flags[3 * z + t1, 3 * ch + u].astype(F32)
        return ints[:, cols] * jnp.where(above, f0, f1)

    def pack(g):
        for u in range(3):
            to = slice(u * TILE, (u + 1) * TILE)
            if g in (0, 4):
                v = masked(chunk(4 - g, 0), u)
                came[g, b, 1, :, to] = v[0:8]
                came[g, b, 2, 0:4, to] = v[8:12]
                came[g, b, 2, 4:8, to] = v[8:12]
            else:
                v = masked(chunk(4 - g, odd), u)
                came[g, b, odd, :, to] = v[0:8]
                came[g, b, 2, 0:4, to] = v[8:12]
                v = masked(chunk(4 - g, 1 - odd), u)
                came[g, b, 1 - odd, :, to] = v[0:8]
                came[g, b, 2, 4:8, to] = v[8:12]

    for g in range(5):
        pack(g)

    def phase1(g, t, slot):
        rows = came.at[g, slot, pl.ds(1, 2)] if g in (0, 4) else came.at[g, slot]
        return remote(rows, rows, s1.at[g, t - 1], r1.at[g, slot], at(0, 0, t, core))

    def start1(g):
        for t in (2, 1, 3):
            phase1(g, t, b).start()

    def phase2(g, o, t):
        src = gath.at[g, core, a] if o == 0 else relay.at[g]
        return remote(src, gath.at[g, core, a], s2.at[g, o, t], r2.at[g, core, a], at(0, t, 0, core + o - 2 * core * o))

    def phase2_came(g, o, t):
        c, slot = (core, lax.rem(a + t, 4)) if o == 0 else (1 - core, lax.rem(b + t, 4))
        device = at(0, t, 0, c) if o == 0 else at(0, 0, t, c)
        return remote(gath.at[g, c, slot], gath.at[g, c, slot], s2.at[g, o, t], r2.at[g, c, slot], device)

    same, other = ((0, 2), (0, 1), (0, 3)), ((1, 2), (1, 1), (1, 3), (1, 0))
    low = lax.broadcasted_iota(I32, (8, W), 0) < 4
    mine_first = (lax.broadcasted_iota(I32, (8, W), 0) < 4) == (core == 0)

    def split_by_core(g, ours, theirs):
        pl.when(core == g // 4)(ours)
        pl.when(core != g // 4)(theirs)

    def start2(g):
        for t in (1, 3, 2):
            phase1(g, t, lax.rem(b + t, 4)).wait_recv()
        for i in range(4):
            gath[g, core, a, i] = came[g, i, 1 if g in (0, 4) else core]
            relay[g, i] = came[g, i, 1 if g in (0, 4) else 1 - core]
        for i in range(2):
            even, uneven = came[g, 2 * i, 2], came[g, 2 * i + 1, 2]
            if g in (0, 4):
                tail = jnp.where(low, even, uneven) if g == 0 else jnp.where(low, uneven, even)
                gath[g, core, a, 4 + i] = tail
                relay[g, 4 + i] = tail
            else:
                gath[g, core, a, 4 + i] = jnp.where(mine_first, even, uneven)
                relay[g, 4 + i] = jnp.where(mine_first, uneven, even)
        if g in (0, 4):
            split_by_core(
                g,
                lambda: [phase2(g, o, t).start() for o, t in same] and None,
                lambda: [phase2(g, o, t).start() for o, t in other] and None,
            )
        else:
            for o, t in ((0, 2), (1, 2), (0, 1), (1, 1), (0, 3), (1, 3), (1, 0)):
                phase2(g, o, t).start()

    def arrived(g):
        return
        for o, t in same + other:
            phase2_came(g, o, t).wait_recv()

    lam_copy = remote(lam, lamx, sl, rl, at(0, 0, 0, 1 - core))

    pl.semaphore_wait(barrier, len(peers))
    start1(0)
    start1(1)

    loads[2].wait()
    loads[3].wait()
    kept = jnp.concatenate([keep[...].astype(F32), jnp.zeros((5, ROWS), F32)], axis=0).T
    for u in range(3):
        cols = slice(u * TILE, (u + 1) * TILE)
        lam[:, cols] = lam[:, cols] * kept[:, u : u + 1]
    lam_copy.start()
    start1(2)
    start1(3)
    start1(4)

    n = lax.broadcasted_iota(I32, (1, W), 1)
    origin = (n >= 192).astype(I32)
    n = n - 192 * origin
    ia = (n * 1366) >> 16
    n = n - 48 * ia
    tile, r = n >> 3, n & 7
    half = r >> 2
    ib = jnp.where(tile < 4, tile, 2 * (tile - 4) + half + core - 2 * core * half)
    chip = jnp.where(origin == 0, ia * 4 + ib, ib * 4 + ia)
    place = 24 * chip + 12 * origin + jnp.where(tile < 4, r, 8 + (r & 3))
    order = (lax.broadcasted_iota(I32, (W, W), 0) == place).astype(BF16)

    def prepare(values, h):
        rows = slice(h * ROWS, (h + 1) * ROWS)
        l1, l2, l3 = (jnp.dot(s, order, preferred_element_type=F32).astype(BF16) for s in split3(values))
        for i, s in enumerate((l1, l1, l1, l3)):
            la[rows, i * W : (i + 1) * W] = s
        for i in range(2):
            lb[rows, i * W : (i + 1) * W] = l2

    prepare(lam[...], 0)
    for g in range(4):
        start2(g)
    lam_copy.wait_recv()
    prepare(lamx[...], 1)

    def right(g):
        for o, t in ((0, 0), (1, 0), (0, 1), (0, 3), (1, 1), (1, 3), (0, 2), (1, 2)):
            c, slot = (core, lax.rem(a + t, 4)) if o == 0 else (1 - core, lax.rem(b + t, 4))
            if o or t:
                phase2_came(g, o, t).wait_recv()
            r1_, r2_, r3_ = split3(gath[g, c, slot].reshape(48, W))
            for k, s in enumerate((r1_, r2_, r3_, r1_)):
                ra[pl.ds(pl.multiple_of(k * W + (c * 4 + slot) * 48, 16), 48)] = s

    def product(h):
        rows = slice(h * ROWS, (h + 1) * ROWS)
        most = jnp.dot(la[rows], ra[...], preferred_element_type=F32)
        return most + jnp.dot(lb[rows], ra[0 : 2 * W], preferred_element_type=F32)

    def sends(j, h, u):
        if j < 3:
            target = at(step, 0, 0, core) if j else at(1 - 2 * h, 0, 0, h)
            hh = h if j else 0
            to = (rq.at[j, hh, u], rs.at[j, hh, u], rzq.at[j, hh, u], rzs.at[j, hh, u])
        else:
            target = at(step, 0, 0, core if h == 0 else 1 - core)
            to = (fq.at[core, u], fs.at[core, u], rfq.at[core, u], rfs.at[core, u])
        return (
            remote(sq.at[j, h, u], to[0], szq.at[j, h, u], to[2], target),
            remote(ss.at[j, h, u], to[1], szs.at[j, h, u], to[3], target),
        )

    def came_in(q_ref, s_ref, q_sem, s_sem):
        for ref, sem in ((q_ref, q_sem), (s_ref, s_sem)):
            remote(ref, ref, szq.at[3, 0, 0], sem, at(step, 0, 0, core)).wait_recv()
        return decode(q_ref[...], s_ref[...])

    def pass_on(j, h, u, add):
        v = part[(h * 2 + u) * SUB : (h * 2 + u + 1) * SUB]
        if add:
            at_ = (j - 1, h, u)
            v = v + came_in(rq.at[at_], rs.at[at_], rzq.at[at_], rzs.at[at_])
        code, scale = encode(v)
        sq[j, h, u] = code
        ss[j, h, u] = scale
        for copy in sends(j, h, u):
            copy.start()

    own_copy = remote(part.at[pl.ds(ROWS, ROWS)], result, so, ro, at(0, 0, 0, 1 - core))

    @pl.when(core == 0)
    def _():
        arrived(0)
        right(0)
        for h in (1, 0):
            part[h * ROWS : (h + 1) * ROWS] = product(h)
            for u in range(2):
                pass_on(0, h, u, False)

    start2(4)

    for j in (1, 2, 3):
        arrived(j)
        right(j)
        for h in (1, 0):
            part[h * ROWS : (h + 1) * ROWS] = product(h)
            for u in range(2):
                pass_on(j, h, u, j > 1 or h == 0)

    @pl.when(core == 1)
    def _():
        arrived(4)
        right(4)
        part[ROWS : 2 * ROWS] = product(1)
        own_copy.start()
        result[...] = product(0)

    lam_copy.wait_send()
    for g in range(5):
        for t in (1, 2, 3):
            phase1(g, t, b).wait_send()
        if g in (0, 4):
            split_by_core(
                g,
                lambda: [phase2(g, o, t).wait_send() for o, t in same] and None,
                lambda: [phase2(g, o, t).wait_send() for o, t in other] and None,
            )
        else:
            for o, t in same + other:
                phase2(g, o, t).wait_send()

    @pl.when(core == 0)
    def _():
        for h in range(2):
            for u in range(2):
                for copy in sends(0, h, u):
                    copy.wait_send()

    for j in (1, 2):
        for h in range(2):
            for u in range(2):
                for copy in sends(j, h, u):
                    copy.wait_send()

    @pl.when(core == 0)
    def _():
        own_copy.wait_recv()

    for u in range(2):
        rows = slice(u * SUB, (u + 1) * SUB)
        v = result[rows]
        for c in range(2):
            at_ = (c, u)
            v = v + came_in(fq.at[at_], fs.at[at_], rfq.at[at_], rfs.at[at_])
        out_hbm[rows] = v

    @pl.when(core == 1)
    def _():
        own_copy.wait_send()

    for h in range(2):
        for u in range(2):
            for copy in sends(3, h, u):
                copy.wait_send()


def per_device(lambda_amp, lambda_tiles, integrals, integral_tiles):
    dma = pltpu.SemaphoreType.DMA
    hbm = pl.BlockSpec(memory_space=pl.ANY)
    return pl.pallas_call(
        kernel,
        out_shape=pltpu.VMEM((ROWS, W), F32),
        in_specs=[hbm] * 4,
        out_specs=pl.BlockSpec(memory_space=pltpu.VMEM),
        scratch_shapes=[
            pltpu.VMEM((ROWS, W), F32),
            pltpu.VMEM((3, ROWS), I32),
            pltpu.VMEM((12, 8 * W), F32),
            pltpu.SMEM((24, 24), I32),
            pltpu.VMEM((ROWS, W), F32),
            pltpu.VMEM((5, 4, 3, 8, W), F32),
            pltpu.VMEM((5, 6, 8, W), F32),
            pltpu.VMEM((5, 2, 4, 6, 8, W), F32),
            pltpu.VMEM((2 * ROWS, 4 * W), BF16),
            pltpu.VMEM((2 * ROWS, 2 * W), BF16),
            pltpu.VMEM((4 * W, W), BF16),
            pltpu.VMEM((2 * ROWS, W), F32),
            pltpu.VMEM((ROWS, W), F32),
            pltpu.VMEM((ROWS, W), F32),
            pltpu.VMEM((4, 2, 2, SUB, W), I16),
            pltpu.VMEM((4, 2, 2, 1, W), F32),
            pltpu.VMEM((3, 2, 2, SUB, W), I16),
            pltpu.VMEM((3, 2, 2, 1, W), F32),
            pltpu.VMEM((2, 2, SUB, W), I16),
            pltpu.VMEM((2, 2, 1, W), F32),
            dma((4,)),
            dma((2,)),
            dma((5, 3)),
            dma((5, 4)),
            dma((5, 2, 4)),
            dma((5, 2, 4)),
            dma,
            dma,
            dma,
            dma,
            dma((4, 2, 2)),
            dma((4, 2, 2)),
            dma((3, 2, 2)),
            dma((3, 2, 2)),
            dma((2, 2)),
            dma((2, 2)),
        ],
        compiler_params=pltpu.CompilerParams(
            collective_id=0, has_side_effects=True, vmem_limit_bytes=48 << 20
        ),
        cost_estimate=pl.CostEstimate(flops=3_700_000_000, bytes_accessed=1_500_000, transcendentals=0),
    )(*(pltpu.with_memory_space_constraint(v, pltpu.HBM) for v in (lambda_amp, lambda_tiles.T, integrals, integral_tiles)))


def solution(mesh):
    placed = (P("own", "rep"), P("own", "rep"), P(("rep", "own"), None), P())
    return jax.shard_map(
        per_device, mesh=mesh, in_specs=placed, out_specs=P("own", "rep"), check_vma=False
    )
```

```python
import jax
import jax.numpy as jnp
from jax import lax
from jax.experimental import pallas as pl
from jax.experimental.pallas import tpu as pltpu
from jax.sharding import PartitionSpec as P

MESH = pl.DeviceIdType.MESH
F32, BF16, I32, I16 = jnp.float32, jnp.bfloat16, jnp.int32, jnp.int16
TILE = 128
W = 384
ROWS = 256
SUB = 128
Q = 32767.0


def split3(v):
    first = v.astype(BF16)
    rest = v - first.astype(F32)
    second = rest.astype(BF16)
    rest = rest - second.astype(F32)
    return first, second, rest.astype(BF16)


def encode(v):
    top = jnp.maximum(jnp.max(jnp.abs(v), axis=0, keepdims=True), 1e-30)
    code = jnp.round(v * (Q / top)).astype(I32).astype(I16)
    return code, top * (1.0 / Q)


def decode(code, scale):
    return code.astype(I32).astype(F32) * scale


def kernel(
    lam_hbm, keep_hbm, ints_hbm, flags_hbm, out_hbm,
    lam, keep, ints, flags, lamx, came, relay, gath, la, lb, ra, part, result, total,
    sq, ss, rq, rs, fq, fs,
    in_sem, out_sem, s1, r1, s2, r2, sl, rl, so, ro, szq, szs, rzq, rzs, rfq, rfs,
):
    z = lax.axis_index("rep")
    own = lax.axis_index("own")
    core = lax.rem(own, 2)
    x = own // 8
    y = lax.rem(own // 2, 4)
    a = x + core * (y - x)
    b = y + core * (x - y)
    step = 1 - 2 * core

    def at(dz, da, db, c):
        aa, bb = lax.rem(a + da, 4), lax.rem(b + db, 4)
        xx, yy = aa + core * (bb - aa), bb + core * (aa - bb)
        return (lax.rem(z + dz + 8, 8), (xx * 4 + yy) * 2 + c)

    def chunk(distance, c):
        return lax.rem(z + distance * (1 - 2 * c) + 8, 8)

    def remote(src, dst, send, recv, device):
        return pltpu.make_async_remote_copy(
            src_ref=src, dst_ref=dst, send_sem=send, recv_sem=recv, device_id=device, device_id_type=MESH
        )

    barrier = pltpu.get_barrier_semaphore()
    peers = [at(0, t, 0, c) for t in (2, 1, 3) for c in (core, 1 - core)]
    peers += [at(0, 0, t, c) for t in (2, 1, 3) for c in (core, 1 - core)]
    peers += [at(d, 0, 0, c) for d in (1, -1) for c in (core, 1 - core)] + [at(0, 0, 0, 1 - core)]
    for peer in peers:
        pl.semaphore_signal(barrier, inc=1, device_id=peer, device_id_type=MESH)

    loads = [
        pltpu.make_async_copy(ints_hbm, ints, in_sem.at[0]),
        pltpu.make_async_copy(flags_hbm, flags, in_sem.at[1]),
        pltpu.make_async_copy(lam_hbm, lam, in_sem.at[2]),
        pltpu.make_async_copy(keep_hbm, keep, in_sem.at[3]),
    ]
    for load in loads:
        load.start()
    loads[0].wait()
    loads[1].wait()

    first_row = own * 12
    t0 = first_row // TILE
    t1 = (first_row + 11) // TILE
    bound = (t0 + 1) * TILE - first_row
    above = lax.broadcasted_iota(I32, (12, TILE), 0) < bound
    odd = lax.rem(b, 2)

    def masked(ch, u):
        cols = pl.ds(pl.multiple_of(ch * W + u * TILE, TILE), TILE)
        f0 = flags[3 * z + t0, 3 * ch + u].astype(F32)
        f1 = flags[3 * z + t1, 3 * ch + u].astype(F32)
        return ints[:, cols] * jnp.where(above, f0, f1)

    def pack(g):
        for u in range(3):
            to = slice(u * TILE, (u + 1) * TILE)
            if g in (0, 4):
                v = masked(chunk(4 - g, 0), u)
                came[g, b, 1, :, to] = v[0:8]
                came[g, b, 2, 0:4, to] = v[8:12]
                came[g, b, 2, 4:8, to] = v[8:12]
            else:
                v = masked(chunk(4 - g, odd), u)
                came[g, b, odd, :, to] = v[0:8]
                came[g, b, 2, 0:4, to] = v[8:12]
                v = masked(chunk(4 - g, 1 - odd), u)
                came[g, b, 1 - odd, :, to] = v[0:8]
                came[g, b, 2, 4:8, to] = v[8:12]

    pack(0)
    pack(1)

    def phase1(g, t, slot):
        rows = came.at[g, slot, pl.ds(1, 2)] if g in (0, 4) else came.at[g, slot]
        return remote(rows, rows, s1.at[g, t - 1], r1.at[g, slot], at(0, 0, t, core))

    def start1(g):
        for t in (2, 1, 3):
            phase1(g, t, b).start()

    def phase2(g, o, t):
        src = gath.at[g, core, a] if o == 0 else relay.at[g]
        return remote(src, gath.at[g, core, a], s2.at[g, o, t], r2.at[g, core, a], at(0, t, 0, core + o - 2 * core * o))

    def phase2_came(g, o, t):
        c, slot = (core, lax.rem(a + t, 4)) if o == 0 else (1 - core, lax.rem(b + t, 4))
        device = at(0, t, 0, c) if o == 0 else at(0, 0, t, c)
        return remote(gath.at[g, c, slot], gath.at[g, c, slot], s2.at[g, o, t], r2.at[g, c, slot], device)

    same, other = ((0, 2), (0, 1), (0, 3)), ((1, 2), (1, 1), (1, 3), (1, 0))
    low = lax.broadcasted_iota(I32, (8, W), 0) < 4
    mine_first = (lax.broadcasted_iota(I32, (8, W), 0) < 4) == (core == 0)

    def split_by_core(g, ours, theirs):
        pl.when(core == g // 4)(ours)
        pl.when(core != g // 4)(theirs)

    def start2(g):
        for t in (1, 3, 2):
            phase1(g, t, lax.rem(b + t, 4)).wait_recv()
        for i in range(4):
            gath[g, core, a, i] = came[g, i, 1 if g in (0, 4) else core]
            relay[g, i] = came[g, i, 1 if g in (0, 4) else 1 - core]
        for i in range(2):
            even, uneven = came[g, 2 * i, 2], came[g, 2 * i + 1, 2]
            if g in (0, 4):
                tail = jnp.where(low, even, uneven) if g == 0 else jnp.where(low, uneven, even)
                gath[g, core, a, 4 + i] = tail
                relay[g, 4 + i] = tail
            else:
                gath[g, core, a, 4 + i] = jnp.where(mine_first, even, uneven)
                relay[g, 4 + i] = jnp.where(mine_first, uneven, even)
        if g in (0, 4):
            split_by_core(
                g,
                lambda: [phase2(g, o, t).start() for o, t in same] and None,
                lambda: [phase2(g, o, t).start() for o, t in other] and None,
            )
        else:
            for o, t in ((0, 2), (1, 2), (0, 1), (1, 1), (0, 3), (1, 3), (1, 0)):
                phase2(g, o, t).start()

    lam_copy = remote(lam, lamx, sl, rl, at(0, 0, 0, 1 - core))

    pl.semaphore_wait(barrier, len(peers))
    start1(0)
    start1(1)
    for g in (2, 3, 4):
        pack(g)
        start1(g)

    loads[2].wait()
    loads[3].wait()
    kept = jnp.concatenate([keep[...].astype(F32), jnp.zeros((5, ROWS), F32)], axis=0).T
    for u in range(3):
        cols = slice(u * TILE, (u + 1) * TILE)
        lam[:, cols] = lam[:, cols] * kept[:, u : u + 1]
    lam_copy.start()

    n = lax.broadcasted_iota(I32, (1, W), 1)
    origin = (n >= 192).astype(I32)
    n = n - 192 * origin
    ia = (n * 1366) >> 16
    n = n - 48 * ia
    tile, r = n >> 3, n & 7
    half = r >> 2
    ib = jnp.where(tile < 4, tile, 2 * (tile - 4) + half + core - 2 * core * half)
    chip = jnp.where(origin == 0, ia * 4 + ib, ib * 4 + ia)
    place = 24 * chip + 12 * origin + jnp.where(tile < 4, r, 8 + (r & 3))
    order = (lax.broadcasted_iota(I32, (W, W), 0) == place).astype(BF16)

    def prepare(values, h):
        rows = slice(h * ROWS, (h + 1) * ROWS)
        l1, l2, l3 = (jnp.dot(s, order, preferred_element_type=F32).astype(BF16) for s in split3(values))
        for i, s in enumerate((l1, l1, l1, l3)):
            la[rows, i * W : (i + 1) * W] = s
        for i in range(2):
            lb[rows, i * W : (i + 1) * W] = l2

    prepare(lam[...], 0)
    for g in range(3):
        start2(g)
    lam_copy.wait_recv()
    prepare(lamx[...], 1)

    def right(g):
        for o, t in ((0, 0), (1, 0), (0, 1), (0, 3), (1, 1), (1, 3), (0, 2), (1, 2)):
            c, slot = (core, lax.rem(a + t, 4)) if o == 0 else (1 - core, lax.rem(b + t, 4))
            if o or t:
                phase2_came(g, o, t).wait_recv()
            r1_, r2_, r3_ = split3(gath[g, c, slot].reshape(48, W))
            for k, s in enumerate((r1_, r2_, r3_, r1_)):
                ra[pl.ds(pl.multiple_of(k * W + (c * 4 + slot) * 48, 16), 48)] = s

    def product(h):
        rows = slice(h * ROWS, (h + 1) * ROWS)
        most = jnp.dot(la[rows], ra[...], preferred_element_type=F32)
        return most + jnp.dot(lb[rows], ra[0 : 2 * W], preferred_element_type=F32)

    def sends(j, h, u):
        if j < 3:
            target = at(step, 0, 0, core) if j else at(1 - 2 * h, 0, 0, h)
            hh = h if j else 0
            to = (rq.at[j, hh, u], rs.at[j, hh, u], rzq.at[j, hh, u], rzs.at[j, hh, u])
        else:
            target = at(step, 0, 0, core if h == 0 else 1 - core)
            to = (fq.at[core, u], fs.at[core, u], rfq.at[core, u], rfs.at[core, u])
        return (
            remote(sq.at[j, h, u], to[0], szq.at[j, h, u], to[2], target),
            remote(ss.at[j, h, u], to[1], szs.at[j, h, u], to[3], target),
        )

    def came_in(q_ref, s_ref, q_sem, s_sem):
        for ref, sem in ((q_ref, q_sem), (s_ref, s_sem)):
            remote(ref, ref, szq.at[3, 0, 0], sem, at(step, 0, 0, core)).wait_recv()
        return decode(q_ref[...], s_ref[...])

    def pass_on(j, h, u, add):
        v = part[(h * 2 + u) * SUB : (h * 2 + u + 1) * SUB]
        if add:
            at_ = (j - 1, h, u)
            v = v + came_in(rq.at[at_], rs.at[at_], rzq.at[at_], rzs.at[at_])
        code, scale = encode(v)
        sq[j, h, u] = code
        ss[j, h, u] = scale
        for copy in sends(j, h, u):
            copy.start()

    own_copy = remote(part.at[pl.ds(ROWS, ROWS)], result, so, ro, at(0, 0, 0, 1 - core))

    @pl.when(core == 0)
    def _():
        right(0)
        for h in (1, 0):
            part[h * ROWS : (h + 1) * ROWS] = product(h)
            for u in range(2):
                pass_on(0, h, u, False)

    start2(3)
    start2(4)

    for j in (1, 2, 3):
        right(j)
        for h in (1, 0):
            part[h * ROWS : (h + 1) * ROWS] = product(h)
            for u in range(2):
                pass_on(j, h, u, j > 1 or h == 0)

    @pl.when(core == 1)
    def _():
        right(4)
        part[ROWS : 2 * ROWS] = product(1)
        own_copy.start()
        result[...] = product(0)

    lam_copy.wait_send()
    for g in range(5):
        for t in (1, 2, 3):
            phase1(g, t, b).wait_send()
        if g in (0, 4):
            split_by_core(
                g,
                lambda: [phase2(g, o, t).wait_send() for o, t in same] and None,
                lambda: [phase2(g, o, t).wait_send() for o, t in other] and None,
            )
        else:
            for o, t in same + other:
                phase2(g, o, t).wait_send()

    @pl.when(core == 0)
    def _():
        for h in range(2):
            for u in range(2):
                for copy in sends(0, h, u):
                    copy.wait_send()

    for j in (1, 2):
        for h in range(2):
            for u in range(2):
                for copy in sends(j, h, u):
                    copy.wait_send()

    @pl.when(core == 0)
    def _():
        own_copy.wait_recv()

    for u in range(2):
        rows = slice(u * SUB, (u + 1) * SUB)
        v = result[rows]
        for c in range(2):
            at_ = (c, u)
            v = v + came_in(fq.at[at_], fs.at[at_], rfq.at[at_], rfs.at[at_])
        out_hbm[rows] = v

    @pl.when(core == 1)
    def _():
        own_copy.wait_send()

    for h in range(2):
        for u in range(2):
            for copy in sends(3, h, u):
                copy.wait_send()


def per_device(lambda_amp, lambda_tiles, integrals, integral_tiles):
    dma = pltpu.SemaphoreType.DMA
    hbm = pl.BlockSpec(memory_space=pl.ANY)
    return pl.pallas_call(
        kernel,
        out_shape=pltpu.VMEM((ROWS, W), F32),
        in_specs=[hbm] * 4,
        out_specs=pl.BlockSpec(memory_space=pltpu.VMEM),
        scratch_shapes=[
            pltpu.VMEM((ROWS, W), F32),
            pltpu.VMEM((3, ROWS), I32),
            pltpu.VMEM((12, 8 * W), F32),
            pltpu.SMEM((24, 24), I32),
            pltpu.VMEM((ROWS, W), F32),
            pltpu.VMEM((5, 4, 3, 8, W), F32),
            pltpu.VMEM((5, 6, 8, W), F32),
            pltpu.VMEM((5, 2, 4, 6, 8, W), F32),
            pltpu.VMEM((2 * ROWS, 4 * W), BF16),
            pltpu.VMEM((2 * ROWS, 2 * W), BF16),
            pltpu.VMEM((4 * W, W), BF16),
            pltpu.VMEM((2 * ROWS, W), F32),
            pltpu.VMEM((ROWS, W), F32),
            pltpu.VMEM((ROWS, W), F32),
            pltpu.VMEM((4, 2, 2, SUB, W), I16),
            pltpu.VMEM((4, 2, 2, 1, W), F32),
            pltpu.VMEM((3, 2, 2, SUB, W), I16),
            pltpu.VMEM((3, 2, 2, 1, W), F32),
            pltpu.VMEM((2, 2, SUB, W), I16),
            pltpu.VMEM((2, 2, 1, W), F32),
            dma((4,)),
            dma((2,)),
            dma((5, 3)),
            dma((5, 4)),
            dma((5, 2, 4)),
            dma((5, 2, 4)),
            dma,
            dma,
            dma,
            dma,
            dma((4, 2, 2)),
            dma((4, 2, 2)),
            dma((3, 2, 2)),
            dma((3, 2, 2)),
            dma((2, 2)),
            dma((2, 2)),
        ],
        compiler_params=pltpu.CompilerParams(
            collective_id=0, has_side_effects=True, vmem_limit_bytes=48 << 20
        ),
        cost_estimate=pl.CostEstimate(flops=3_700_000_000, bytes_accessed=1_500_000, transcendentals=0),
    )(*(pltpu.with_memory_space_constraint(v, pltpu.HBM) for v in (lambda_amp, lambda_tiles.T, integrals, integral_tiles)))


def solution(mesh):
    placed = (P("own", "rep"), P("own", "rep"), P(("rep", "own"), None), P())
    return jax.shard_map(
        per_device, mesh=mesh, in_specs=placed, out_specs=P("own", "rep"), check_vma=False
    )
```

```python
import jax
import jax.numpy as jnp
from jax import lax
from jax.experimental import pallas as pl
from jax.experimental.pallas import tpu as pltpu
from jax.sharding import PartitionSpec as P

MESH = pl.DeviceIdType.MESH
F32, BF16, I32, I16 = jnp.float32, jnp.bfloat16, jnp.int32, jnp.int16
TILE = 128
W = 384
ROWS = 256
SUB = 128
Q = 32767.0


def split3(v):
    first = v.astype(BF16)
    rest = v - first.astype(F32)
    second = rest.astype(BF16)
    rest = rest - second.astype(F32)
    return first, second, rest.astype(BF16)


def encode(v):
    top = jnp.maximum(jnp.max(jnp.abs(v), axis=0, keepdims=True), 1e-30)
    code = jnp.round(v * (Q / top)).astype(I32).astype(I16)
    return code, top * (1.0 / Q)


def decode(code, scale):
    return code.astype(I32).astype(F32) * scale


def kernel(
    lam_hbm, keep_hbm, ints_hbm, flags_hbm, out_hbm,
    lam, keep, ints, flags, lamx, came, relay, gath, la, lb, ra, part, result, total,
    sq, ss, rq, rs,
    in_sem, out_sem, s1, r1, s2, r2, sl, rl, so, ro, szq, szs, rzq, rzs,
):
    z = lax.axis_index("rep")
    own = lax.axis_index("own")
    core = lax.rem(own, 2)
    x = own // 8
    y = lax.rem(own // 2, 4)
    a = x + core * (y - x)
    b = y + core * (x - y)
    step = 1 - 2 * core

    def at(dz, da, db, c):
        aa, bb = lax.rem(a + da, 4), lax.rem(b + db, 4)
        xx, yy = aa + core * (bb - aa), bb + core * (aa - bb)
        return (lax.rem(z + dz + 8, 8), (xx * 4 + yy) * 2 + c)

    def chunk(distance, c):
        return lax.rem(z + distance * (1 - 2 * c) + 8, 8)

    def remote(src, dst, send, recv, device):
        return pltpu.make_async_remote_copy(
            src_ref=src, dst_ref=dst, send_sem=send, recv_sem=recv, device_id=device, device_id_type=MESH
        )

    barrier = pltpu.get_barrier_semaphore()
    peers = [at(0, t, 0, 1 - core) for t in range(4)] + [at(0, 0, t, 1 - core) for t in (1, 2, 3)]
    peers += [at(0, t, 0, core) for t in (1, 2, 3)] + [at(0, 0, t, core) for t in (1, 2, 3)]
    peers += [at(d, 0, 0, c) for d in (1, -1) for c in (core, 1 - core)]
    for peer in peers:
        pl.semaphore_signal(barrier, inc=1, device_id=peer, device_id_type=MESH)

    loads = [
        pltpu.make_async_copy(ints_hbm, ints, in_sem.at[0]),
        pltpu.make_async_copy(flags_hbm, flags, in_sem.at[1]),
        pltpu.make_async_copy(lam_hbm, lam, in_sem.at[2]),
        pltpu.make_async_copy(keep_hbm, keep, in_sem.at[3]),
    ]
    for load in loads:
        load.start()
    loads[0].wait()
    loads[1].wait()

    first_row = own * 12
    t0 = first_row // TILE
    t1 = (first_row + 11) // TILE
    bound = (t0 + 1) * TILE - first_row
    above = lax.broadcasted_iota(I32, (12, TILE), 0) < bound
    odd = lax.rem(b, 2)

    def masked(ch, u):
        cols = pl.ds(pl.multiple_of(ch * W + u * TILE, TILE), TILE)
        f0 = flags[3 * z + t0, 3 * ch + u].astype(F32)
        f1 = flags[3 * z + t1, 3 * ch + u].astype(F32)
        return ints[:, cols] * jnp.where(above, f0, f1)

    def pack(g):
        for u in range(3):
            to = slice(u * TILE, (u + 1) * TILE)
            if g in (0, 4):
                v = masked(chunk(4 - g, 0), u)
                came[g, b, 1, :, to] = v[0:8]
                came[g, b, 2, 0:4, to] = v[8:12]
                came[g, b, 2, 4:8, to] = v[8:12]
            else:
                v = masked(chunk(4 - g, odd), u)
                came[g, b, odd, :, to] = v[0:8]
                came[g, b, 2, 0:4, to] = v[8:12]
                v = masked(chunk(4 - g, 1 - odd), u)
                came[g, b, 1 - odd, :, to] = v[0:8]
                came[g, b, 2, 4:8, to] = v[8:12]

    for g in range(5):
        pack(g)

    def phase1(g, t, slot):
        rows = came.at[g, slot, pl.ds(1, 2)] if g in (0, 4) else came.at[g, slot]
        return remote(rows, rows, s1.at[g, t - 1], r1.at[g, slot], at(0, 0, t, core))

    def start1(g):
        for t in (2, 1, 3):
            phase1(g, t, b).start()

    def phase2(g, o, t):
        src = gath.at[g, core, a] if o == 0 else relay.at[g]
        return remote(src, gath.at[g, core, a], s2.at[g, o, t], r2.at[g, core, a], at(0, t, 0, core + o - 2 * core * o))

    def phase2_came(g, o, t):
        c, slot = (core, lax.rem(a + t, 4)) if o == 0 else (1 - core, lax.rem(b + t, 4))
        device = at(0, t, 0, c) if o == 0 else at(0, 0, t, c)
        return remote(gath.at[g, c, slot], gath.at[g, c, slot], s2.at[g, o, t], r2.at[g, c, slot], device)

    same, other = ((0, 2), (0, 1), (0, 3)), ((1, 2), (1, 1), (1, 3), (1, 0))
    low = lax.broadcasted_iota(I32, (8, W), 0) < 4
    mine_first = (lax.broadcasted_iota(I32, (8, W), 0) < 4) == (core == 0)

    def split_by_core(g, ours, theirs):
        pl.when(core == g // 4)(ours)
        pl.when(core != g // 4)(theirs)

    def start2(g):
        for t in (1, 3, 2):
            phase1(g, t, lax.rem(b + t, 4)).wait_recv()
        for i in range(4):
            gath[g, core, a, i] = came[g, i, 1 if g in (0, 4) else core]
            relay[g, i] = came[g, i, 1 if g in (0, 4) else 1 - core]
        for i in range(2):
            even, uneven = came[g, 2 * i, 2], came[g, 2 * i + 1, 2]
            if g in (0, 4):
                tail = jnp.where(low, even, uneven) if g == 0 else jnp.where(low, uneven, even)
                gath[g, core, a, 4 + i] = tail
                relay[g, 4 + i] = tail
            else:
                gath[g, core, a, 4 + i] = jnp.where(mine_first, even, uneven)
                relay[g, 4 + i] = jnp.where(mine_first, uneven, even)
        if g in (0, 4):
            split_by_core(
                g,
                lambda: [phase2(g, o, t).start() for o, t in same] and None,
                lambda: [phase2(g, o, t).start() for o, t in other] and None,
            )
        else:
            for o, t in ((0, 2), (1, 2), (0, 1), (1, 1), (0, 3), (1, 3), (1, 0)):
                phase2(g, o, t).start()

    lam_copy = remote(lam, lamx, sl, rl, at(0, 0, 0, 1 - core))

    pl.semaphore_wait(barrier, len(peers))
    start1(0)
    start1(1)

    loads[2].wait()
    loads[3].wait()
    kept = jnp.concatenate([keep[...].astype(F32), jnp.zeros((5, ROWS), F32)], axis=0).T
    for u in range(3):
        cols = slice(u * TILE, (u + 1) * TILE)
        lam[:, cols] = lam[:, cols] * kept[:, u : u + 1]
    lam_copy.start()
    start1(2)
    start1(3)
    start1(4)

    n = lax.broadcasted_iota(I32, (1, W), 1)
    origin = (n >= 192).astype(I32)
    n = n - 192 * origin
    ia = (n * 1366) >> 16
    n = n - 48 * ia
    tile, r = n >> 3, n & 7
    half = r >> 2
    ib = jnp.where(tile < 4, tile, 2 * (tile - 4) + half + core - 2 * core * half)
    chip = jnp.where(origin == 0, ia * 4 + ib, ib * 4 + ia)
    place = 24 * chip + 12 * origin + jnp.where(tile < 4, r, 8 + (r & 3))
    order = (lax.broadcasted_iota(I32, (W, W), 0) == place).astype(BF16)

    def prepare(values, h):
        rows = slice(h * ROWS, (h + 1) * ROWS)
        l1, l2, l3 = (jnp.dot(s, order, preferred_element_type=F32).astype(BF16) for s in split3(values))
        for i, s in enumerate((l1, l1, l1, l3)):
            la[rows, i * W : (i + 1) * W] = s
        for i in range(2):
            lb[rows, i * W : (i + 1) * W] = l2

    prepare(lam[...], 0)
    for g in range(4):
        start2(g)
    lam_copy.wait_recv()
    prepare(lamx[...], 1)

    def right(g):
        for o, t in ((0, 0), (1, 0), (0, 1), (0, 3), (1, 1), (1, 3), (0, 2), (1, 2)):
            c, slot = (core, lax.rem(a + t, 4)) if o == 0 else (1 - core, lax.rem(b + t, 4))
            if o or t:
                phase2_came(g, o, t).wait_recv()
            r1_, r2_, r3_ = split3(gath[g, c, slot].reshape(48, W))
            for k, s in enumerate((r1_, r2_, r3_, r1_)):
                ra[pl.ds(pl.multiple_of(k * W + (c * 4 + slot) * 48, 16), 48)] = s

    def product(h):
        rows = slice(h * ROWS, (h + 1) * ROWS)
        most = jnp.dot(la[rows], ra[...], preferred_element_type=F32)
        return most + jnp.dot(lb[rows], ra[0 : 2 * W], preferred_element_type=F32)

    def sends(j, h, u):
        if isinstance(j, int) and j == 0:
            target, hh = at(1 - 2 * h, 0, 0, h), 0
        else:
            last = j // 3
            target = at(step, 0, 0, core + last * h * (1 - 2 * core))
            hh = h + last * (core - h)
        return (
            remote(sq.at[j, h, u], rq.at[j, hh, u], szq.at[j, h, u], rzq.at[j, hh, u], target),
            remote(ss.at[j, h, u], rs.at[j, hh, u], szs.at[j, h, u], rzs.at[j, hh, u], target),
        )

    def came_in(j, h, u):
        for ref, sem in ((rq, rzq), (rs, rzs)):
            remote(ref.at[j, h, u], ref.at[j, h, u], szq.at[3, 0, 0], sem.at[j, h, u], at(step, 0, 0, core)).wait_recv()

    def pass_on(j, h, u):
        v = part[(h * 2 + u) * SUB : (h * 2 + u + 1) * SUB]
        if not isinstance(j, int):
            if h == 1:
                pl.when(j > 1)(lambda: came_in(j - 1, h, u))
            else:
                came_in(j - 1, h, u)
            v = v + decode(rq[j - 1, h, u], rs[j - 1, h, u])
        code, scale = encode(v)
        sq[j, h, u] = code
        ss[j, h, u] = scale
        for copy in sends(j, h, u):
            copy.start()

    rq[0, 1] = jnp.zeros((2, SUB, W), I16)
    rs[0, 1] = jnp.zeros((2, 1, W), F32)

    own_copy = remote(part.at[pl.ds(ROWS, ROWS)], result, so, ro, at(0, 0, 0, 1 - core))

    @pl.when(core == 0)
    def _():
        right(0)
        for h in (1, 0):
            part[h * ROWS : (h + 1) * ROWS] = product(h)
            for u in range(2):
                pass_on(0, h, u)

    start2(4)

    def ring_step(j, carry):
        right(j)
        for h in (1, 0):
            part[h * ROWS : (h + 1) * ROWS] = product(h)
            for u in range(2):
                pass_on(j, h, u)
        return carry

    lax.fori_loop(1, 4, ring_step, 0)

    @pl.when(core == 1)
    def _():
        right(4)
        part[ROWS : 2 * ROWS] = product(1)
        own_copy.start()
        result[...] = product(0)

    lam_copy.wait_send()
    for g in range(5):
        for t in (1, 2, 3):
            phase1(g, t, b).wait_send()
        if g in (0, 4):
            split_by_core(
                g,
                lambda: [phase2(g, o, t).wait_send() for o, t in same] and None,
                lambda: [phase2(g, o, t).wait_send() for o, t in other] and None,
            )
        else:
            for o, t in same + other:
                phase2(g, o, t).wait_send()

    @pl.when(core == 0)
    def _():
        for h in range(2):
            for u in range(2):
                for copy in sends(0, h, u):
                    copy.wait_send()

    for j in (1, 2):
        for h in range(2):
            for u in range(2):
                for copy in sends(j, h, u):
                    copy.wait_send()

    @pl.when(core == 0)
    def _():
        own_copy.wait_recv()

    for u in range(2):
        rows = slice(u * SUB, (u + 1) * SUB)
        v = result[rows]
        for c in range(2):
            came_in(3, c, u)
            v = v + decode(rq[3, c, u], rs[3, c, u])
        out_hbm[rows] = v

    @pl.when(core == 1)
    def _():
        own_copy.wait_send()

    for h in range(2):
        for u in range(2):
            for copy in sends(3, h, u):
                copy.wait_send()


def per_device(lambda_amp, lambda_tiles, integrals, integral_tiles):
    dma = pltpu.SemaphoreType.DMA
    hbm = pl.BlockSpec(memory_space=pl.ANY)
    return pl.pallas_call(
        kernel,
        out_shape=pltpu.VMEM((ROWS, W), F32),
        in_specs=[hbm] * 4,
        out_specs=pl.BlockSpec(memory_space=pltpu.VMEM),
        scratch_shapes=[
            pltpu.VMEM((ROWS, W), F32),
            pltpu.VMEM((3, ROWS), I32),
            pltpu.VMEM((12, 8 * W), F32),
            pltpu.SMEM((24, 24), I32),
            pltpu.VMEM((ROWS, W), F32),
            pltpu.VMEM((5, 4, 3, 8, W), F32),
            pltpu.VMEM((5, 6, 8, W), F32),
            pltpu.VMEM((5, 2, 4, 6, 8, W), F32),
            pltpu.VMEM((2 * ROWS, 4 * W), BF16),
            pltpu.VMEM((2 * ROWS, 2 * W), BF16),
            pltpu.VMEM((4 * W, W), BF16),
            pltpu.VMEM((2 * ROWS, W), F32),
            pltpu.VMEM((ROWS, W), F32),
            pltpu.VMEM((ROWS, W), F32),
            pltpu.VMEM((4, 2, 2, SUB, W), I16),
            pltpu.VMEM((4, 2, 2, 1, W), F32),
            pltpu.VMEM((4, 2, 2, SUB, W), I16),
            pltpu.VMEM((4, 2, 2, 1, W), F32),
            dma((4,)),
            dma((2,)),
            dma((5, 3)),
            dma((5, 4)),
            dma((5, 2, 4)),
            dma((5, 2, 4)),
            dma,
            dma,
            dma,
            dma,
            dma((4, 2, 2)),
            dma((4, 2, 2)),
            dma((4, 2, 2)),
            dma((4, 2, 2)),
        ],
        compiler_params=pltpu.CompilerParams(
            collective_id=0, has_side_effects=True, vmem_limit_bytes=48 << 20
        ),
        cost_estimate=pl.CostEstimate(flops=3_700_000_000, bytes_accessed=1_500_000, transcendentals=0),
    )(*(pltpu.with_memory_space_constraint(v, pltpu.HBM) for v in (lambda_amp, lambda_tiles.T, integrals, integral_tiles)))


def solution(mesh):
    placed = (P("own", "rep"), P("own", "rep"), P(("rep", "own"), None), P())
    return jax.shard_map(
        per_device, mesh=mesh, in_specs=placed, out_specs=P("own", "rep"), check_vma=False
    )
```
